32 devices in a mesh: row: 4 (over y, core), col: 8 (over z, x).
Axes of the slice: x: 2, y: 2, z: 4, core: 2. Of those that a mesh axis runs over, the one named last changes fastest.
Arguments:
- object_field: float32 [2, 1024, 2048], P(None, 'row', 'col'), may hold values from -6 to 6
- probe_field: float32 [2, 2, 128, 128], replicated, may hold values from -6 to 6
- amplitudes: float32 [4, 8, 24, 128, 128], P('row', 'col'), may hold values from 0.3 to 6
- offsets: int32 [4, 8, 24, 2], P('row', 'col'), may hold values from -64 to 191
- counts: int32 [4, 8], P('row', 'col'), may hold values from 1 to 24, as said below
Outputs:
- object_next: float32 [2, 1024, 2048], P(None, 'row', 'col')
- probe_next: float32 [2, 2, 128, 128], replicated
The draws below stay inside these ranges and needn't reach their ends.
Inputs may be any that keep to these rules, and one draw needn't show every extreme that they name: `counts`: slots at and above a tile's count are unused; some tile has all 24 slots live.
All inputs are finite; a program needn't handle non-finite values.
Results may differ from the reference program's by a relative error of at most 0.0001.
Values sent between devices are 32-bit elements; how exact they have to be, the bound alone decides.
No kernel may reach another device: no remote copies, remote signals or barrier semaphores. Data moves between devices by JAX's collectives and lax.ppermute only.
A program may use at most 64 MiB of HBM per device.

```python
import math
import jax
import jax.numpy as jnp
from jax import lax

PSIZE = 128
MODES = 2
PASSES = 2
TILE = 256
CAP = 24
HALF = 64
NR = 1024
NC = 2048
SLOTS = 768
N_ROW = 4
N_COL = 8


def draw_counts(key, part):
    col_index = jnp.arange(N_COL, dtype=jnp.int32)
    ceiling = (CAP + 2 * CAP * col_index // max(N_COL - 1, 1)) // 3
    ceiling = jnp.maximum(ceiling, 1)
    first_key = jax.random.fold_in(key, 11)
    second_key = jax.random.fold_in(key, 23)
    drawn = jax.random.randint(first_key, (N_ROW, N_COL), 0, 1 << 20)
    result = 1 + drawn % ceiling[None, :]
    chosen = jax.random.randint(second_key, (), 0, N_ROW)
    return result.at[chosen, N_COL - 1].set(CAP).astype(jnp.int32)


def with_ends(values, key, smallest, top_value):
    spot = [jax.random.randint(jax.random.fold_in(key, axis), (), 0, length) for axis, length in enumerate(values.shape)]
    longest = values.shape.index(max(values.shape))
    next_to = spot[:longest] + [(spot[longest] + 1) % values.shape[longest]] + spot[longest + 1:]
    return values.at[tuple(spot)].set(smallest).at[tuple(next_to)].set(top_value)


def steps_of(key, extent, pieces, low, largest):
    level, own = 1.0, jax.random.fold_in(key, 6)
    for dim, shards_of in pieces:
        draws = jnp.exp(jax.random.uniform(jax.random.fold_in(own, dim), (shards_of,), jnp.float32, low / len(pieces), largest / len(pieces)))
        level = level * jnp.repeat(draws, extent[dim] // shards_of).reshape([-1 if axis == dim else 1 for axis in range(len(extent))])
    return level


def centred(rng, dims, width, reach, cuts=(), kind=jnp.bfloat16):
    loudness = steps_of(rng, dims, cuts, -0.22, 0.18) if cuts else 1.0
    values = jax.random.normal(rng, dims, jnp.float32) * width * loudness
    return jnp.minimum(jnp.maximum(values, -reach), reach).astype(kind)


def setup_inputs(seed: int = 0) -> dict:
    key_list = jax.random.split(jax.random.key(seed), 6)
    object_field = centred(key_list[0], (2, NR, NC), 1.0, 6.0, ((1, 4), (2, 8)), jnp.float32)
    probe_field = centred(key_list[1], (2, MODES, PSIZE, PSIZE), 1.0, 6.0, (), jnp.float32)
    amplitudes = jnp.clip(jnp.exp(math.log(6.0) - 2.9957322 * jax.random.uniform(key_list[2], (N_ROW, N_COL, CAP, PSIZE, PSIZE), jnp.float32) ** steps_of(key_list[2], (N_ROW, N_COL, CAP, PSIZE, PSIZE), ((0, 4), (1, 8)), -0.2, 0.2)), 0.3, 6.0)
    offsets = with_ends(jax.random.randint(key_list[3], (N_ROW, N_COL, CAP, 2), 0 - HALF, TILE - HALF), jax.random.fold_in(key_list[3], 1), 0 - HALF, (TILE - HALF) - 1).astype(jnp.int32)
    counts = draw_counts(jax.random.fold_in(key_list[5], 71), 0)
    return dict(object_field=object_field, probe_field=probe_field, amplitudes=amplitudes, offsets=offsets, counts=counts)


EPSILON = 1e-06

def exit_change(window, probe, amplitude):
    psi = probe * window[None]
    spectrum = jnp.fft.fft2(psi, norm='ortho')
    total = lax.optimization_barrier(jnp.sum(jnp.real(spectrum) ** 2 + jnp.imag(spectrum) ** 2, axis=0))
    factor = amplitude / jnp.maximum(jnp.sqrt(total), 1.0)
    revised = jnp.fft.ifft2(spectrum * factor[None], norm='ortho')
    return revised - psi

def reference(object_field, probe_field, amplitudes, offsets, counts):
    probe = lax.complex(probe_field[0], probe_field[1])
    power = lax.optimization_barrier(jnp.sum(probe_field[0] ** 2 + probe_field[1] ** 2, axis=0))
    regular = 0.1 * jnp.max(power) + EPSILON
    slot_index = jnp.arange(CAP, dtype=jnp.int32)
    live = (slot_index[None, None, :] < counts[:, :, None]).astype(power.dtype)
    tile_rows = (jnp.arange(N_ROW, dtype=jnp.int32) * TILE)[:, None, None]
    tile_cols = (jnp.arange(N_COL, dtype=jnp.int32) * TILE)[None, :, None]
    start_rows = (offsets[..., 0] + tile_rows + HALF).reshape(-1).astype(jnp.int32)
    start_cols = (offsets[..., 1] + tile_cols + HALF).reshape(-1).astype(jnp.int32)
    flat_amps = amplitudes.reshape(-1, PSIZE, PSIZE)
    flat_live = live.reshape(-1)
    current = object_field
    gradient = jnp.zeros_like(probe)
    for pass_index in range(PASSES):
        padded = jnp.pad(current, ((0, 0), (HALF, HALF), (HALF, HALF)))
        numer_init = jnp.zeros((3,) + padded.shape[1:], power.dtype)

        def visit(carry, item):
            numer, grad = carry
            row_start, col_start, amplitude, alive = item
            zero = jnp.zeros((), jnp.int32)
            block = lax.dynamic_slice(padded, (zero, row_start, col_start), (2, PSIZE, PSIZE))
            window = lax.complex(block[0], block[1])
            change = exit_change(window, probe, amplitude) * alive
            object_term = lax.optimization_barrier(jnp.sum(jnp.conj(probe) * change, axis=0))
            patch = jnp.stack([jnp.real(object_term), jnp.imag(object_term), power * alive])
            before = lax.dynamic_slice(numer, (zero, row_start, col_start), (3, PSIZE, PSIZE))
            numer = lax.dynamic_update_slice(numer, before + patch, (zero, row_start, col_start))
            mean_power = jnp.mean(block[0] ** 2 + block[1] ** 2) + EPSILON
            grad = grad + jnp.conj(window)[None] * change / mean_power
            return ((numer, grad), None)
        (numer, gradient), _ = lax.scan(visit, (numer_init, gradient), (start_rows, start_cols, flat_amps, flat_live))
        inner = numer[:, HALF:HALF + NR, HALF:HALF + NC]
        current = current + inner[:2] / (inner[2:3] + regular)
    probe_new = probe + gradient / SLOTS
    return (current, jnp.stack([jnp.real(probe_new), jnp.imag(probe_new)]))
```

```python
import functools

import jax
import jax.numpy as jnp
import ml_dtypes
import numpy as np
from jax import lax
from jax.experimental import pallas as pl
from jax.experimental.pallas import tpu as pltpu
from jax.sharding import PartitionSpec as P

PASSES = 2
EPSILON = 1e-06
VMEM_BYTES = 48 * 1024 * 1024
ROWS = 32


def split(values):
    high = values.astype(jnp.bfloat16)
    low = (values - high.astype(jnp.float32)).astype(jnp.bfloat16)
    return high, low


def tables(size):
    positions = np.arange(size)
    angles = 2.0 * np.pi / size * (positions[:, None] * positions[None, :] % size)
    cosine = np.cos(angles) / np.sqrt(size)
    sine = np.sin(angles) / np.sqrt(size)
    minus = np.block([[cosine, sine], [-sine, cosine]]).astype(np.float32)
    plus = np.block([[cosine, -sine], [sine, cosine]]).astype(np.float32)
    parts = []
    for table in (minus, plus):
        high = table.astype(ml_dtypes.bfloat16)
        low = (table - high.astype(np.float32)).astype(ml_dtypes.bfloat16)
        parts += [high, low]
    return jnp.asarray(np.stack(parts))


def corner(offset_ref, slot, margin, lanes):
    row = offset_ref[slot, 0] + margin
    col = offset_ref[slot, 1] + margin
    return row, col // lanes, lax.rem(col, lanes)


def add_rolled(sums, channel, row, tile, shift, lane, values):
    rows, lanes = values.shape
    rolled = pltpu.roll(values, shift, 1)
    inside = lane >= shift
    where = pl.ds(row, rows)
    zero = jnp.zeros_like(rolled)
    sums[channel, tile, where, :] += jnp.where(inside, rolled, zero)
    sums[channel, tile + 1, where, :] += jnp.where(inside, zero, rolled)


def weight_kernel(margin, count_ref, offset_ref, probe_ref, weight_ref, power_ref):
    size = probe_ref.shape[-1]
    weight_ref[...] = jnp.zeros_like(weight_ref)
    power_ref[...] = jnp.sum(probe_ref[...] ** 2, axis=(0, 1))

    def visit(slot, carry):
        row, tile, shift = corner(offset_ref, slot, margin, size)
        for first in range(0, size, ROWS):
            lane = lax.broadcasted_iota(jnp.int32, (ROWS, size), 1)
            add_rolled(weight_ref, 0, row + first, tile, shift, lane, power_ref[pl.ds(first, ROWS), :])
        return carry

    lax.fori_loop(0, count_ref[0, 0], visit, 0)


def handle(slots, margin, offset_ref, amp_ref, probe_ref, table_ref, object_ref, sums_ref, gradient_ref, work):
    windows, psis, in_high, in_low, row_high, row_low, spec_high, spec_low, back_high, back_low, scales = work
    size = probe_ref.shape[-1]
    many = len(slots)
    minus_high, minus_low, plus_high, plus_low = (table_ref[i] for i in range(4))
    lane = lax.broadcasted_iota(jnp.int32, (ROWS, size), 1)
    places = [corner(offset_ref, slot, margin, size) for slot in slots]

    for j, (row, tile, shift) in enumerate(places):
        norm = jnp.zeros((8, size), jnp.float32)
        for first in range(0, size, ROWS):
            where = pl.ds(row + first, ROWS)
            own = pl.ds(first, ROWS)
            window = []
            for part in range(2):
                both = jnp.where(
                    lane >= shift, object_ref[part, tile, where, :], object_ref[part, tile + 1, where, :]
                )
                value = pltpu.roll(both, lax.rem(size - shift, size), 1)
                windows[j, part, own, :] = value
                window.append(value)
            norm += jnp.sum((window[0] ** 2 + window[1] ** 2).reshape(ROWS // 8, 8, size), axis=0)
            for mode in range(2):
                real, imag = probe_ref[0, mode, own, :], probe_ref[1, mode, own, :]
                psi = (real * window[0] - imag * window[1], real * window[1] + imag * window[0])
                cols = slice((2 * j + mode) * size, (2 * j + mode + 1) * size)
                for part in range(2):
                    psis[j, part, mode, own, :] = psi[part]
                    high, low = split(psi[part])
                    in_high[pl.ds(part * size + first, ROWS), cols] = high
                    in_low[pl.ds(part * size + first, ROWS), cols] = low
        mean = jnp.sum(jnp.sum(norm, axis=0, keepdims=True), axis=1, keepdims=True) / (size * size)
        scales[j] = jnp.broadcast_to(1.0 / (mean + EPSILON), (8, size))

    wide = many * 2 * size

    def left(high, low, x_high, x_low):
        table = jnp.concatenate([high, high, low], axis=1)
        h = x_high[:, :wide]
        return jnp.dot(table, jnp.concatenate([h, x_low[:, :wide], h], axis=0), preferred_element_type=jnp.float32)

    def right(high, low, x_high, x_low):
        table = jnp.concatenate([high, high, low], axis=0)
        h = x_high[:wide, :]
        return jnp.dot(jnp.concatenate([h, x_low[:wide, :], h], axis=1), table, preferred_element_type=jnp.float32)

    half = left(minus_high, minus_low, in_high, in_low)
    for j in range(many):
        for mode in range(2):
            k = (2 * j + mode) * size
            for part in range(2):
                for first in range(0, size, ROWS):
                    value = half[part * size + first : part * size + first + ROWS, k : k + size]
                    high, low = split(value)
                    where = (pl.ds(k + first, ROWS), slice(part * size, (part + 1) * size))
                    row_high[where] = high
                    row_low[where] = low
    spectrum = right(plus_high, plus_low, row_high, row_low)
    for j, slot in enumerate(slots):
        for first in range(0, size, ROWS):
            values = {}
            for mode in range(2):
                k = (2 * j + mode) * size + first
                for part in range(2):
                    values[mode, part] = spectrum[k : k + ROWS, part * size : (part + 1) * size]
            total = sum(value**2 for value in values.values())
            factor = amp_ref[slot, pl.ds(first, ROWS), :] * lax.rsqrt(jnp.maximum(total, 1.0))
            for (mode, part), value in values.items():
                high, low = split(value * factor)
                where = (pl.ds((2 * j + mode) * size + first, ROWS), slice(part * size, (part + 1) * size))
                spec_high[where] = high
                spec_low[where] = low
    half = right(minus_high, minus_low, spec_high, spec_low)
    for j in range(many):
        for mode in range(2):
            k = (2 * j + mode) * size
            for part in range(2):
                for first in range(0, size, ROWS):
                    value = half[k + first : k + first + ROWS, part * size : (part + 1) * size]
                    high, low = split(value)
                    where = (pl.ds(part * size + first, ROWS), slice(k, k + size))
                    back_high[where] = high
                    back_low[where] = low
    revised = left(plus_high, plus_low, back_high, back_low)
    for first in range(0, size, ROWS):
        own = pl.ds(first, ROWS)
        gradient = {}
        for j, (row, tile, shift) in enumerate(places):
            scale = jnp.concatenate([scales[j]] * (ROWS // 8), axis=0)
            window = [windows[j, part, own, :] for part in range(2)]
            scaled = [value * scale for value in window]
            numer_real = numer_imag = 0.0
            for mode in range(2):
                k = (2 * j + mode) * size
                real = revised[first : first + ROWS, k : k + size] - psis[j, 0, mode, own, :]
                imag = revised[size + first : size + first + ROWS, k : k + size] - psis[j, 1, mode, own, :]
                p_real, p_imag = probe_ref[0, mode, own, :], probe_ref[1, mode, own, :]
                numer_real += p_real * real + p_imag * imag
                numer_imag += p_real * imag - p_imag * real
                gradient[0, mode] = gradient.get((0, mode), 0.0) + (scaled[0] * real + scaled[1] * imag)
                gradient[1, mode] = gradient.get((1, mode), 0.0) + (scaled[0] * imag - scaled[1] * real)
            add_rolled(sums_ref, 0, row + first, tile, shift, lane, numer_real)
            add_rolled(sums_ref, 1, row + first, tile, shift, lane, numer_imag)
        for (part, mode), value in gradient.items():
            gradient_ref[part, mode, own, :] += value


def visit_all(count_ref, margin, offset_ref, *rest):
    count = count_ref[0, 0]

    def pair(i, carry):
        handle([2 * i, 2 * i + 1], margin, offset_ref, *rest)
        return carry

    lax.fori_loop(0, count // 2, pair, 0)

    @pl.when(lax.rem(count, 2) == 1)
    def _():
        handle([count - 1], margin, offset_ref, *rest)


def first_kernel(margin, count_ref, offset_ref, amp_ref, probe_ref, table_ref, object_ref, sums_ref, gradient_ref, *work):
    sums_ref[...] = jnp.zeros_like(sums_ref)
    gradient_ref[...] = jnp.zeros_like(gradient_ref)
    visit_all(count_ref, margin, offset_ref, amp_ref, probe_ref, table_ref, object_ref, sums_ref, gradient_ref, work)


def next_kernel(margin, count_ref, offset_ref, amp_ref, probe_ref, table_ref, object_ref, gradient_in, sums_ref, gradient_ref, *work):
    sums_ref[...] = jnp.zeros_like(sums_ref)
    gradient_ref[...] = gradient_in[...]
    visit_all(count_ref, margin, offset_ref, amp_ref, probe_ref, table_ref, object_ref, sums_ref, gradient_ref, work)


def vmem():
    return pl.BlockSpec(memory_space=pltpu.VMEM)


def smem():
    return pl.BlockSpec(memory_space=pltpu.SMEM)


def run_pass(margin, counts, offsets, amplitudes, probe, table, extended, gradient):
    size = probe.shape[-1]
    bf16 = jnp.bfloat16
    scratch = [
        pltpu.VMEM((2, 2, size, size), jnp.float32),
        pltpu.VMEM((2, 2, 2, size, size), jnp.float32),
        pltpu.VMEM((2 * size, 4 * size), bf16),
        pltpu.VMEM((2 * size, 4 * size), bf16),
        pltpu.VMEM((4 * size, 2 * size), bf16),
        pltpu.VMEM((4 * size, 2 * size), bf16),
        pltpu.VMEM((4 * size, 2 * size), bf16),
        pltpu.VMEM((4 * size, 2 * size), bf16),
        pltpu.VMEM((2 * size, 4 * size), bf16),
        pltpu.VMEM((2 * size, 4 * size), bf16),
        pltpu.VMEM((2, 8, size), jnp.float32),
    ]
    out_shape = [
        jax.ShapeDtypeStruct(extended.shape, jnp.float32),
        jax.ShapeDtypeStruct(probe.shape, jnp.float32),
    ]
    arguments = [counts, offsets, amplitudes, probe, table, extended]
    body = first_kernel
    if gradient is not None:
        arguments.append(gradient)
        body = next_kernel
    return pl.pallas_call(
        functools.partial(body, margin),
        out_shape=out_shape,
        in_specs=[smem(), smem()] + [vmem()] * (len(arguments) - 2),
        out_specs=[vmem(), vmem()],
        scratch_shapes=scratch,
        compiler_params=pltpu.CompilerParams(vmem_limit_bytes=VMEM_BYTES),
        cost_estimate=pl.CostEstimate(flops=10**10, bytes_accessed=10**7, transcendentals=0),
    )(*arguments)


def shifted(value, axis, steps):
    count = lax.axis_size(axis)
    initial, last = max(0, -steps), min(count, count - steps)
    return lax.ppermute(value, axis, [(source, source + steps) for source in range(initial, last)])


def to_tiles(array, lanes):
    channels, rows, cols = array.shape
    return jnp.transpose(array.reshape(channels, rows, cols // lanes, lanes), (0, 2, 1, 3))


def from_tiles(array):
    channels, tiles, rows, lanes = array.shape
    return jnp.transpose(array, (0, 2, 1, 3)).reshape(channels, rows, tiles * lanes)


def complete(sums, size):
    top, middle, bottom = sums[:, :, :size], sums[:, :, size:-size], sums[:, :, -size:]
    from_above = shifted(bottom, "row", 1)
    from_below = shifted(top, "row", -1)
    sums = jnp.concatenate([top + from_above, middle, bottom + from_below], axis=2)
    from_left = shifted(sums[:, -1], "col", 1)
    from_right = shifted(sums[:, 0], "col", -1)
    return jnp.concatenate(
        [sums[:, :1] + from_left[:, None], sums[:, 1:-1], sums[:, -1:] + from_right[:, None]], axis=1
    )


def all_sum(value):
    total = value.reshape(-1, value.shape[-1])
    steps = []
    for axis in ("row", "col"):
        distance = 1
        while distance < lax.axis_size(axis):
            steps.append((axis, distance))
            distance *= 2

    def swap(part, axis, distance):
        return lax.ppermute(part, axis, [(i, i ^ distance) for i in range(lax.axis_size(axis))])

    for axis, distance in steps:
        bit = lax.axis_index(axis) // distance % 2
        half = total.shape[0] // 2
        sent = lax.dynamic_slice_in_dim(total, (1 - bit) * half, half, 0)
        kept = lax.dynamic_slice_in_dim(total, bit * half, half, 0)
        total = kept + swap(sent, axis, distance)
    for axis, distance in reversed(steps):
        bit = lax.axis_index(axis) // distance % 2
        other = swap(total, axis, distance)
        total = jnp.where(
            bit == 0, jnp.concatenate([total, other], axis=0), jnp.concatenate([other, total], axis=0)
        )
    return total.reshape(value.shape)


def local(object_field, probe, amplitudes, offsets, counts):
    size = probe.shape[2]
    margin = size // 2
    slot_total = amplitudes.shape[2]
    amplitudes, offsets = amplitudes[0, 0], offsets[0, 0]
    table = tables(size)
    tile_rows, tile_cols = object_field.shape[1:]
    extent_rows, extent_cols = tile_rows + 2 * margin, tile_cols + 2 * margin

    weight, power = pl.pallas_call(
        functools.partial(weight_kernel, margin),
        out_shape=[
            jax.ShapeDtypeStruct((1, extent_cols // size, extent_rows, size), jnp.float32),
            jax.ShapeDtypeStruct((size, size), jnp.float32),
        ],
        in_specs=[smem(), smem(), vmem()],
        out_specs=[vmem(), vmem()],
        compiler_params=pltpu.CompilerParams(vmem_limit_bytes=VMEM_BYTES),
        cost_estimate=pl.CostEstimate(flops=10**7, bytes_accessed=10**7, transcendentals=0),
    )(counts, offsets, probe)
    regular = 0.1 * jnp.max(power) + EPSILON

    above = shifted(object_field[:, -margin:], "row", 1)
    below = shifted(object_field[:, :margin], "row", -1)
    tall = jnp.concatenate([above, object_field, below], axis=1)
    left = shifted(tall[:, :, -margin:], "col", 1)
    right = shifted(tall[:, :, :margin], "col", -1)
    current = to_tiles(jnp.concatenate([left, tall, right], axis=2), size)

    row_index, col_index = lax.axis_index("row"), lax.axis_index("col")
    rows = row_index * tile_rows + jnp.arange(extent_rows, dtype=jnp.int32) - margin
    cols = col_index * tile_cols + jnp.arange(extent_cols, dtype=jnp.int32) - margin
    rows_in = (rows >= 0) & (rows < tile_rows * lax.axis_size("row"))
    cols_in = (cols >= 0) & (cols < tile_cols * lax.axis_size("col"))
    inside = (rows_in[None, :, None] & cols_in.reshape(-1, 1, size))[None]

    weight = complete(weight, size)
    inverse = jnp.where(inside, 1.0 / (weight + regular), 0.0)

    gradient = None
    for _ in range(PASSES):
        sums, gradient = run_pass(margin, counts, offsets, amplitudes, probe, table, current, gradient)
        current = current + complete(sums, size) * inverse

    object_next = from_tiles(current)[:, margin:-margin, margin:-margin]
    divisor = float(lax.axis_size("row") * lax.axis_size("col") * slot_total)
    return object_next, probe + all_sum(gradient) / divisor


def solution(mesh):
    in_specs = (
        P(None, "row", "col"),
        P(),
        P("row", "col", None, None, None),
        P("row", "col", None, None),
        P("row", "col"),
    )
    out_specs = (P(None, "row", "col"), P())
    return jax.shard_map(local, mesh=mesh, in_specs=in_specs, out_specs=out_specs, check_vma=False)
```

```python
import functools

import jax
import jax.numpy as jnp
import ml_dtypes
import numpy as np
from jax import lax
from jax.experimental import pallas as pl
from jax.experimental.pallas import tpu as pltpu
from jax.sharding import PartitionSpec as P

EPSILON = 1e-06
VMEM_BYTES = 24 * 1024 * 1024
ROWS = 32


def split(values):
    high = values.astype(jnp.bfloat16)
    low = (values - high.astype(jnp.float32)).astype(jnp.bfloat16)
    return high, low


def tables(size):
    positions = np.arange(size)
    angles = 2.0 * np.pi / size * (positions[:, None] * positions[None, :] % size)
    cosine = np.cos(angles) / np.sqrt(size)
    sine = np.sin(angles) / np.sqrt(size)
    minus = np.block([[cosine, sine], [-sine, cosine]]).astype(np.float32)
    plus = np.block([[cosine, -sine], [sine, cosine]]).astype(np.float32)
    parts = []
    for table in (minus, plus):
        high = table.astype(ml_dtypes.bfloat16)
        low = (table - high.astype(np.float32)).astype(ml_dtypes.bfloat16)
        parts += [high, low]
    return jnp.asarray(np.stack(parts))


def corner(offset_ref, slot, margin, base, lanes):
    row = offset_ref[slot, 0] + margin
    col = offset_ref[slot, 1] + margin
    return row, col // lanes - base, lax.rem(col, lanes)


def add_rolled(sums, channel, row, tile, shift, lane, values):
    rows, lanes = values.shape
    rolled = pltpu.roll(values, shift, 1)
    inside = lane >= shift
    where = pl.ds(row, rows)
    zero = jnp.zeros_like(rolled)
    sums[tile, channel, where, :] += jnp.where(inside, rolled, zero)
    sums[tile + 1, channel, where, :] += jnp.where(inside, zero, rolled)


def handle(slots, margin, base, offset_ref, amp_ref, probe_ref, table_ref, object_ref, sums_ref, gradient_ref, work):
    windows, psis, in_high, in_low, row_high, row_low, spec_high, spec_low, back_high, back_low, scales = work
    size = probe_ref.shape[-1]
    many = len(slots)
    minus_high, minus_low, plus_high, plus_low = (table_ref[i] for i in range(4))
    lane = lax.broadcasted_iota(jnp.int32, (ROWS, size), 1)
    places = [corner(offset_ref, slot, margin, base, size) for slot in slots]

    for j, (row, tile, shift) in enumerate(places):
        norm = jnp.zeros((8, size), jnp.float32)
        for first in range(0, size, ROWS):
            where = pl.ds(row + first, ROWS)
            own = pl.ds(first, ROWS)
            window = []
            for part in range(2):
                both = jnp.where(
                    lane >= shift, object_ref[tile, part, where, :], object_ref[tile + 1, part, where, :]
                )
                value = pltpu.roll(both, lax.rem(size - shift, size), 1)
                windows[j, part, own, :] = value
                window.append(value)
            norm += jnp.sum((window[0] ** 2 + window[1] ** 2).reshape(ROWS // 8, 8, size), axis=0)
            for mode in range(2):
                real, imag = probe_ref[0, mode, own, :], probe_ref[1, mode, own, :]
                psi = (real * window[0] - imag * window[1], real * window[1] + imag * window[0])
                cols = slice((2 * j + mode) * size, (2 * j + mode + 1) * size)
                for part in range(2):
                    psis[j, part, mode, own, :] = psi[part]
                    high, low = split(psi[part])
                    in_high[pl.ds(part * size + first, ROWS), cols] = high
                    in_low[pl.ds(part * size + first, ROWS), cols] = low
        mean = jnp.sum(jnp.sum(norm, axis=0, keepdims=True), axis=1, keepdims=True) / (size * size)
        scales[j] = jnp.broadcast_to(1.0 / (mean + EPSILON), (8, size))

    wide = many * 2 * size

    def left(high, low, x_high, x_low):
        table = jnp.concatenate([high, high, low], axis=1)
        h = x_high[:, :wide]
        return jnp.dot(table, jnp.concatenate([h, x_low[:, :wide], h], axis=0), preferred_element_type=jnp.float32)

    def right(high, low, x_high, x_low):
        table = jnp.concatenate([high, high, low], axis=0)
        h = x_high[:wide, :]
        return jnp.dot(jnp.concatenate([h, x_low[:wide, :], h], axis=1), table, preferred_element_type=jnp.float32)

    half = left(minus_high, minus_low, in_high, in_low)
    for j in range(many):
        for mode in range(2):
            k = (2 * j + mode) * size
            for part in range(2):
                for first in range(0, size, ROWS):
                    value = half[part * size + first : part * size + first + ROWS, k : k + size]
                    high, low = split(value)
                    where = (pl.ds(k + first, ROWS), slice(part * size, (part + 1) * size))
                    row_high[where] = high
                    row_low[where] = low
    spectrum = right(plus_high, plus_low, row_high, row_low)
    for j, slot in enumerate(slots):
        for first in range(0, size, ROWS):
            values = {}
            for mode in range(2):
                k = (2 * j + mode) * size + first
                for part in range(2):
                    values[mode, part] = spectrum[k : k + ROWS, part * size : (part + 1) * size]
            total = sum(value**2 for value in values.values())
            factor = amp_ref[slot, pl.ds(first, ROWS), :] * lax.rsqrt(jnp.maximum(total, 1.0))
            for (mode, part), value in values.items():
                high, low = split(value * factor)
                where = (pl.ds((2 * j + mode) * size + first, ROWS), slice(part * size, (part + 1) * size))
                spec_high[where] = high
                spec_low[where] = low
    half = right(minus_high, minus_low, spec_high, spec_low)
    for j in range(many):
        for mode in range(2):
            k = (2 * j + mode) * size
            for part in range(2):
                for first in range(0, size, ROWS):
                    value = half[k + first : k + first + ROWS, part * size : (part + 1) * size]
                    high, low = split(value)
                    where = (pl.ds(part * size + first, ROWS), slice(k, k + size))
                    back_high[where] = high
                    back_low[where] = low
    revised = left(plus_high, plus_low, back_high, back_low)
    for first in range(0, size, ROWS):
        own = pl.ds(first, ROWS)
        gradient = {}
        for j, (row, tile, shift) in enumerate(places):
            scale = jnp.concatenate([scales[j]] * (ROWS // 8), axis=0)
            window = [windows[j, part, own, :] for part in range(2)]
            scaled = [value * scale for value in window]
            numer_real = numer_imag = 0.0
            for mode in range(2):
                k = (2 * j + mode) * size
                real = revised[first : first + ROWS, k : k + size] - psis[j, 0, mode, own, :]
                imag = revised[size + first : size + first + ROWS, k : k + size] - psis[j, 1, mode, own, :]
                p_real, p_imag = probe_ref[0, mode, own, :], probe_ref[1, mode, own, :]
                numer_real += p_real * real + p_imag * imag
                numer_imag += p_real * imag - p_imag * real
                gradient[0, mode] = gradient.get((0, mode), 0.0) + (scaled[0] * real + scaled[1] * imag)
                gradient[1, mode] = gradient.get((1, mode), 0.0) + (scaled[0] * imag - scaled[1] * real)
            add_rolled(sums_ref, 0, row + first, tile, shift, lane, numer_real)
            add_rolled(sums_ref, 1, row + first, tile, shift, lane, numer_imag)
        for (part, mode), value in gradient.items():
            gradient_ref[part, mode, own, :] += value


def weight_kernel(margin, count_ref, offset_ref, probe_ref, weight_ref, power_ref):
    size = probe_ref.shape[-1]
    weight_ref[...] = jnp.zeros_like(weight_ref)
    power_ref[...] = jnp.sum(probe_ref[...] ** 2, axis=(0, 1))
    lane = lax.broadcasted_iota(jnp.int32, (ROWS, size), 1)

    def visit(slot, carry):
        row, tile, shift = corner(offset_ref, slot, margin, 0, size)
        for first in range(0, size, ROWS):
            add_rolled(weight_ref, 0, row + first, tile, shift, lane, power_ref[pl.ds(first, ROWS), :])
        return carry

    lax.fori_loop(0, count_ref[0, 0], visit, 0)


def run_slots(margin, side, count_ref, offset_ref, chosen, *rest):
    size = 2 * margin

    def look(slot, found):
        left = offset_ref[slot, 1] + margin < size
        chosen[found] = slot
        return found + jnp.where(left, 1 - side, side)

    found = lax.fori_loop(0, count_ref[0, 0], look, 0)

    def pair(i, carry):
        handle([chosen[2 * i], chosen[2 * i + 1]], margin, side, offset_ref, *rest)
        return carry

    lax.fori_loop(0, found // 2, pair, 0)

    @pl.when(lax.rem(found, 2) == 1)
    def _():
        handle([chosen[found - 1]], margin, side, offset_ref, *rest)


def lanes_of(shape):
    return lax.broadcasted_iota(jnp.int32, shape, len(shape) - 1)


def turned(value, margin):
    return pltpu.roll(value, margin, 1)


def joined(low, high, margin):
    return jnp.where(lanes_of(low.shape) < margin, turned(low, margin), turned(high, margin))


def packed_low(real, imag, margin):
    return jnp.where(lanes_of(real.shape) < margin, real, turned(imag, margin))


def packed_high(real, imag, margin):
    return jnp.where(lanes_of(real.shape) < margin, turned(real, margin), imag)


def chosen_by(flag, first, second):
    return jnp.where(jnp.full(first.shape, flag, jnp.int32) == 1, first, second)


def extend_kernel(margin, flag_ref, object_ref, a_ref, b_ref, ext_ref, high_ref, low_ref):
    odd = lax.rem(flag_ref[0], 2)
    rows, cols = object_ref.shape[1:]
    size = 2 * margin
    blocks = cols // size
    segments = [(0, margin), (margin, rows), (margin + rows, margin)]
    for number, (first, length) in enumerate(segments):
        where = pl.ds(first, length)
        values = {}
        for part in range(2):
            for block in range(blocks):
                lanes = slice(block * size, (block + 1) * size)
                if number == 0:
                    value = chosen_by(odd, a_ref[part, :, lanes], b_ref[part, :, lanes])
                elif number == 1:
                    value = object_ref[part, :, lanes]
                else:
                    value = chosen_by(odd, b_ref[part, :, lanes], a_ref[part, :, lanes])
                values[part, block] = value
            zero = jnp.zeros((length, size), jnp.float32)
            for tile in range(blocks + 1):
                low = values.get((part, tile - 1), zero)
                high = values.get((part, tile), zero)
                ext_ref[tile, part, where, :] = joined(low, high, margin)
        high_ref[where, :] = packed_high(values[0, blocks - 1], values[1, blocks - 1], margin)
        low_ref[where, :] = packed_low(values[0, 0], values[1, 0], margin)


def first_left_kernel(margin, count, offset, amp, probe, table, ext, halo, weight, message, middle, gradient, ext_left, *work):
    source, sums, chosen, *work = work
    gradient[...] = jnp.zeros_like(gradient)
    sums[...] = jnp.zeros_like(sums)
    edge = halo[...]
    for part, value in enumerate((edge, turned(edge, margin))):
        ext_left[part] = jnp.where(lanes_of(edge.shape) < margin, value, ext[0, part])
        source[0, part] = ext_left[part]
        source[1, part] = ext[1, part]
    run_slots(margin, 0, count, offset, chosen, amp, probe, table, source, sums, gradient, work)
    message[0:2] = sums[0]
    message[2] = weight[0, 0]
    middle[...] = sums[1]


def first_right_kernel(margin, count, offset, amp, probe, table, ext, halo, gradient_in, sums, gradient, ext_right, *work):
    source, chosen, *work = work
    tiles = ext.shape[0]
    gradient[...] = gradient_in[...]
    sums[...] = jnp.zeros_like(sums)
    edge = halo[...]
    for part, value in enumerate((turned(edge, margin), edge)):
        ext_right[part] = jnp.where(lanes_of(edge.shape) < margin, ext[tiles - 1, part], value)
        for tile in range(1, tiles - 1):
            source[tile - 1, part] = ext[tile, part]
        source[tiles - 2, part] = ext_right[part]
    run_slots(margin, 1, count, offset, chosen, amp, probe, table, source, sums, gradient, work)


def gather_kernel(margin, flag_ref, sums, middle, message, weight, received, total, a_ref, b_ref):
    size = 2 * margin
    tiles = total.shape[0]
    rows = total.shape[2]
    total[0] = message[...]
    for tile in range(1, tiles):
        for channel in range(3):
            value = sums[tile - 1, channel] if channel < 2 else weight[tile, 0]
            if tile == 1 and channel < 2:
                value += middle[channel]
            if tile == tiles - 1:
                value += received[channel]
            total[tile, channel] = value
    odd = lax.rem(flag_ref[0], 2)
    down = pl.multiple_of((1 - odd) * (rows - size), 8)
    up = pl.multiple_of(odd * (rows - size), 8)
    for tile in range(tiles):
        for channel in range(3):
            a_ref[tile, channel] = total[tile, channel, pl.ds(down, size), :]
            b_ref[tile, channel] = total[tile, channel, pl.ds(up, size), :]


def update_kernel(margin, flag_ref, probe, total, a_ref, b_ref, ext, ext_left, ext_right, ext_next, last, inverse):
    size = 2 * margin
    tiles, _, rows, _ = total.shape
    row_index, col_index, row_count, col_count = (flag_ref[i] for i in range(4))
    odd = lax.rem(row_index, 2)
    power = jnp.sum(probe[...] ** 2, axis=(0, 1))
    largest = jnp.max(jnp.max(power, axis=0, keepdims=True), axis=1, keepdims=True)
    regular = 0.1 * largest + EPSILON
    inner_rows, inner_cols = rows - size, (tiles - 1) * size
    for first, length in ((0, size), (size, rows - 2 * size), (rows - size, size)):
        where = pl.ds(first, length)
        row = lax.broadcasted_iota(jnp.int32, (length, size), 0) + (first - margin) + row_index * inner_rows
        for tile in range(tiles):
            col = lanes_of((length, size)) + (tile * size - margin) + col_index * inner_cols
            inside = (row >= 0) & (row < row_count * inner_rows) & (col >= 0) & (col < col_count * inner_cols)
            values = [total[tile, channel, where, :] for channel in range(3)]
            for channel in range(3):
                if first == 0:
                    values[channel] += chosen_by(odd, a_ref[tile, channel], b_ref[tile, channel])
                elif first == rows - size:
                    values[channel] += chosen_by(odd, b_ref[tile, channel], a_ref[tile, channel])
            over = 1.0 / (values[2] + regular)
            inverse[tile, where, :] = over
            for part in range(2):
                if tile == 0:
                    before = ext_left[part, where, :]
                elif tile == tiles - 1:
                    before = ext_right[part, where, :]
                else:
                    before = ext[tile, part, where, :]
                after = jnp.where(inside, before + values[part] * over, 0.0)
                ext_next[tile, part, where, :] = after
                if tile == tiles - 1:
                    last[part, where, :] = after


def second_right_kernel(margin, count, offset, amp, probe, table, ext, gradient_in, inverse, sums, gradient, message, *work):
    source, chosen, *work = work
    tiles = ext.shape[0]
    gradient[...] = gradient_in[...]
    sums[...] = jnp.zeros_like(sums)
    source[...] = ext[1:]
    run_slots(margin, 1, count, offset, chosen, amp, probe, table, source, sums, gradient, work)
    message[0] = packed_high(sums[tiles - 2, 0], sums[tiles - 2, 1], margin)
    message[1] = inverse[tiles - 1]


def second_left_kernel(
    margin, count, offset, amp, probe, table, flag_ref, ext, received, gradient_in, sums, message, kept, sent, first, *work
):
    source, gradient, chosen, *work = work
    gradient[...] = gradient_in[...]
    sums[...] = jnp.zeros_like(sums)
    inward = jnp.minimum(flag_ref[1], 1)
    for part in range(2):
        first[part] = chosen_by(inward, received[part], ext[0, part])
        source[0, part] = first[part]
        source[1, part] = ext[1, part]
    run_slots(margin, 0, count, offset, chosen, amp, probe, table, source, sums, gradient, work)
    message[...] = packed_low(sums[0, 0], sums[0, 1], margin)
    odd = lax.rem(flag_ref[0], 2)
    kept[...] = gradient[odd]
    sent[...] = gradient[1 - odd]


def collect_kernel(margin, flag_ref, left, right, from_left, from_right, ext, first, inverse, inner, a_ref, b_ref, base, inv):
    size = 2 * margin
    tiles = ext.shape[0]
    rows = ext.shape[2]
    tall = rows - size
    inward = jnp.minimum(flag_ref[1], 1)
    for part in range(2):
        for block in range(tiles - 1):
            lanes = slice(block * size, (block + 1) * size)

            def tile_sum(tile):
                if tile == 0:
                    return left[0, part]
                return left[1, part] + right[0, part] if tile == 1 else right[tile - 1, part]

            value = joined(tile_sum(block), tile_sum(block + 1), margin)
            lane = lanes_of(value.shape)
            if block == 0:
                edge = from_left[0] if part == 0 else turned(from_left[0], margin)
                value += jnp.where(lane < margin, edge, 0.0)
            if block == tiles - 2:
                edge = turned(from_right[...], margin) if part == 0 else from_right[...]
                value += jnp.where(lane < margin, 0.0, edge)
            inner[part, :, lanes] = value
            own = pl.ds(margin, tall)
            low = first[part, own, :] if block == 0 else ext[block, part, own, :]
            base[part, :, lanes] = joined(low, ext[block + 1, part, own, :], margin)
            if part == 0:
                low = inverse[block, own, :]
                if block == 0:
                    low = chosen_by(inward, from_left[1, own, :], low)
                inv[:, lanes] = joined(low, inverse[block + 1, own, :], margin)
    odd = lax.rem(flag_ref[0], 2)
    down = pl.multiple_of((1 - odd) * (rows - margin), 8)
    up = pl.multiple_of(odd * (rows - margin), 8)
    for part in range(2):
        a_ref[part] = inner[part, pl.ds(down, margin), :]
        b_ref[part] = inner[part, pl.ds(up, margin), :]


def finish_kernel(margin, flag_ref, inner, a_ref, b_ref, base, inv, out):
    odd = lax.rem(flag_ref[0], 2)
    rows = base.shape[1]
    for part in range(2):
        for first, length in ((0, margin), (margin, rows - 2 * margin), (rows - margin, margin)):
            value = inner[part, pl.ds(margin + first, length), :]
            if first == 0:
                value += chosen_by(odd, a_ref[part], b_ref[part])
            elif first == rows - margin:
                value += chosen_by(odd, b_ref[part], a_ref[part])
            where = pl.ds(first, length)
            out[part, where, :] = base[part, where, :] + value * inv[where, :]


def call(kernel, shapes, arguments, scalars, scratch=(), flops=10**7):
    def space(is_scalar):
        return pl.BlockSpec(memory_space=pltpu.SMEM if is_scalar else pltpu.VMEM)

    return pl.pallas_call(
        kernel,
        out_shape=[jax.ShapeDtypeStruct(shape, jnp.float32) for shape in shapes],
        in_specs=[space(i in scalars) for i in range(len(arguments))],
        out_specs=[space(False)] * len(shapes),
        scratch_shapes=list(scratch),
        compiler_params=pltpu.CompilerParams(vmem_limit_bytes=VMEM_BYTES),
        cost_estimate=pl.CostEstimate(flops=flops, bytes_accessed=10**6, transcendentals=0),
    )(*arguments)


def work_scratch(size):
    bf16 = jnp.bfloat16
    tall = pltpu.VMEM((4 * size, 2 * size), bf16)
    wide = pltpu.VMEM((2 * size, 4 * size), bf16)
    return [
        pltpu.VMEM((2, 2, size, size), jnp.float32),
        pltpu.VMEM((2, 2, 2, size, size), jnp.float32),
        wide, wide, tall, tall, tall, tall, wide, wide,
        pltpu.VMEM((2, 8, size), jnp.float32),
    ]


def shifted(value, axis, steps):
    count = lax.axis_size(axis)
    initial, last = max(0, -steps), min(count, count - steps)
    return lax.ppermute(value, axis, [(source, source + steps) for source in range(initial, last)])


def swapped(value, axis, first):
    pairs = []
    for i in range(first, lax.axis_size(axis) - 1, 2):
        pairs += [(i, i + 1), (i + 1, i)]
    return lax.ppermute(value, axis, pairs)


def all_sum(total):
    cols = lax.axis_size("col")
    count = lax.axis_size("row") * cols
    masks = []
    distance = 2
    while distance < lax.axis_size("row"):
        masks.append(distance * cols)
        distance *= 2
    distance = 1
    while distance < cols:
        masks.append(distance)
        distance *= 2

    def partner(mask):
        return lax.ppermute(total, ("row", "col"), [(i, i ^ mask) for i in range(count)])

    while masks:
        near, *masks = masks
        if masks:
            far, *masks = masks
            one, two, three = partner(near), partner(far), partner(near ^ far)
            total = (total + one) + (two + three)
        else:
            total = total + partner(near)
    return total


def local(object_field, probe, amplitudes, offsets, counts):
    size = probe.shape[2]
    margin = size // 2
    slot_total = amplitudes.shape[2]
    amplitudes, offsets = amplitudes[0, 0], offsets[0, 0]
    table = tables(size)
    tile_rows, tile_cols = object_field.shape[1:]
    rows = tile_rows + size
    tiles = tile_cols // size + 1
    row_index, col_index = lax.axis_index("row"), lax.axis_index("col")
    flags = jnp.stack([row_index, col_index, lax.axis_size("row"), lax.axis_size("col")]).astype(jnp.int32)
    odd = row_index % 2 == 1

    upper, lower = object_field[:, :margin], object_field[:, -margin:]
    a_in = swapped(jnp.where(odd, upper, lower), "row", 0)
    b_in = swapped(jnp.where(odd, lower, upper), "row", 1)

    weight, _ = call(
        functools.partial(weight_kernel, margin),
        [(tiles, 1, rows, size), (size, size)],
        [counts, offsets, probe],
        (0, 1),
    )
    ext, high, low = call(
        functools.partial(extend_kernel, margin),
        [(tiles, 2, rows, size), (rows, size), (rows, size)],
        [flags, object_field, a_in, b_in],
        (0,),
    )
    left_halo = shifted(high, "col", 1)
    right_halo = shifted(low, "col", -1)

    common = [counts, offsets, amplitudes, probe, table]
    list_scratch = pltpu.SMEM((slot_total + 1,), jnp.int32)
    work = work_scratch(size)
    two_tiles = pltpu.VMEM((2, 2, rows, size), jnp.float32)
    right_tiles = pltpu.VMEM((tiles - 1, 2, rows, size), jnp.float32)
    column = (2, rows, size)
    heavy = 4 * 10**10

    message, middle, gradient, ext_left = call(
        functools.partial(first_left_kernel, margin),
        [(3, rows, size), column, probe.shape, column],
        common + [ext, left_halo, weight],
        (0, 1),
        [two_tiles, two_tiles, list_scratch] + work,
        heavy,
    )
    from_right = shifted(message, "col", -1)
    sums, gradient, ext_right = call(
        functools.partial(first_right_kernel, margin),
        [(tiles - 1,) + column, probe.shape, column],
        common + [ext, right_halo, gradient],
        (0, 1),
        [right_tiles, list_scratch] + work,
        heavy,
    )
    total, a_out, b_out = call(
        functools.partial(gather_kernel, margin),
        [(tiles, 3, rows, size), (tiles, 3, size, size), (tiles, 3, size, size)],
        [flags, sums, middle, message, weight, from_right],
        (0,),
    )
    a_in = swapped(a_out, "row", 0)
    b_in = swapped(b_out, "row", 1)
    ext, last, inverse = call(
        functools.partial(update_kernel, margin),
        [(tiles,) + column, column, (tiles, rows, size)],
        [flags, probe, total, a_in, b_in, ext, ext_left, ext_right],
        (0,),
    )
    from_left = shifted(last, "col", 1)
    right, gradient, message = call(
        functools.partial(second_right_kernel, margin),
        [(tiles - 1,) + column, probe.shape, column],
        common + [ext, gradient, inverse],
        (0, 1),
        [right_tiles, list_scratch] + work,
        heavy,
    )
    edge_left = shifted(message, "col", 1)
    left, message, kept, sent, first = call(
        functools.partial(second_left_kernel, margin),
        [(2,) + column, (rows, size), probe.shape[1:], probe.shape[1:], column],
        common + [flags, ext, from_left, gradient],
        (0, 1, 5),
        [two_tiles, pltpu.VMEM(probe.shape, jnp.float32), list_scratch] + work,
        heavy,
    )
    edge_right = shifted(message, "col", -1)
    share = all_sum(kept + swapped(sent, "row", 0))

    wide = (2, rows, tile_cols)
    inner, a_out, b_out, base, inv = call(
        functools.partial(collect_kernel, margin),
        [wide, (2, margin, tile_cols), (2, margin, tile_cols), object_field.shape, object_field.shape[1:]],
        [flags, left, right, edge_left, edge_right, ext, first, inverse],
        (0,),
    )
    a_in = swapped(a_out, "row", 0)
    b_in = swapped(b_out, "row", 1)
    (object_next,) = call(
        functools.partial(finish_kernel, margin),
        [object_field.shape],
        [flags, inner, a_in, b_in, base, inv],
        (0,),
    )

    divisor = float(lax.axis_size("row") * lax.axis_size("col") * slot_total)
    share = jnp.where(odd, probe[1], probe[0]) + share / divisor
    other = swapped(share, "row", 0)
    probe_next = jnp.where(odd, jnp.stack([other, share]), jnp.stack([share, other]))
    return object_next, probe_next


def solution(mesh):
    in_specs = (
        P(None, "row", "col"),
        P(),
        P("row", "col", None, None, None),
        P("row", "col", None, None),
        P("row", "col"),
    )
    out_specs = (P(None, "row", "col"), P())
    return jax.shard_map(local, mesh=mesh, in_specs=in_specs, out_specs=out_specs, check_vma=False)
```

```python
import functools

import jax
import jax.numpy as jnp
import ml_dtypes
import numpy as np
from jax import lax
from jax.experimental import pallas as pl
from jax.experimental.pallas import tpu as pltpu
from jax.sharding import PartitionSpec as P

EPSILON = 1e-06
VMEM_BYTES = 24 * 1024 * 1024
ROWS = 32
PER = 4
SKEW = 0
SPLITS = {1: [1], 2: [1, 1], 3: [1, 1, 1], 4: [1, 1, 1, 1]}


def split_of(n):
    return SPLITS[n]


def split(values):
    high = values.astype(jnp.bfloat16)
    low = (values - high.astype(jnp.float32)).astype(jnp.bfloat16)
    return high, low


def tables(size):
    positions = np.arange(size)
    angles = 2.0 * np.pi / size * (positions[:, None] * positions[None, :] % size)
    cosine = np.cos(angles) / np.sqrt(size)
    sine = np.sin(angles) / np.sqrt(size)
    minus = np.block([[cosine, sine], [-sine, cosine]]).astype(np.float32)
    plus = np.block([[cosine, -sine], [sine, cosine]]).astype(np.float32)
    parts = []
    for table in (minus, plus):
        high = table.astype(ml_dtypes.bfloat16)
        low = (table - high.astype(np.float32)).astype(ml_dtypes.bfloat16)
        parts += [high, low]
    return jnp.asarray(np.stack(parts))


def corner(offset_ref, slot, margin, base, lanes):
    row = offset_ref[slot, 0] + margin
    col = offset_ref[slot, 1] + margin
    return row, col // lanes - base, lax.rem(col, lanes)


def add_rolled(sums, channel, row, tile, shift, lane, values):
    rows, lanes = values.shape
    rolled = pltpu.roll(values, shift, 1)
    inside = lane >= shift
    where = pl.ds(row, rows)
    zero = jnp.zeros_like(rolled)
    sums[tile, channel, where, :] += jnp.where(inside, rolled, zero)
    sums[tile + 1, channel, where, :] += jnp.where(inside, zero, rolled)


def stages(slots, margin, base, offset_ref, amp_ref, probe_ref, table_ref, object_ref, sums_ref, gradient_ref, work):
    windows, psis, in_high, in_low, row_high, row_low, spec_high, spec_low, back_high, back_low, scales = work
    size = probe_ref.shape[-1]
    many = len(slots)
    minus_high, minus_low, plus_high, plus_low = (table_ref[i] for i in range(4))
    lane = lax.broadcasted_iota(jnp.int32, (ROWS, size), 1)
    places = [corner(offset_ref, slot, margin, base, size) for slot in slots]

    for j, (row, tile, shift) in enumerate(places):
        norm = jnp.zeros((8, size), jnp.float32)
        for first in range(0, size, ROWS):
            where = pl.ds(row + first, ROWS)
            own = pl.ds(first, ROWS)
            window = []
            for part in range(2):
                both = jnp.where(
                    lane >= shift, object_ref[tile, part, where, :], object_ref[tile + 1, part, where, :]
                )
                value = pltpu.roll(both, lax.rem(size - shift, size), 1)
                windows[j, part, own, :] = value
                window.append(value)
            norm += jnp.sum((window[0] ** 2 + window[1] ** 2).reshape(ROWS // 8, 8, size), axis=0)
            for mode in range(2):
                real, imag = probe_ref[0, mode, own, :], probe_ref[1, mode, own, :]
                psi = (real * window[0] - imag * window[1], real * window[1] + imag * window[0])
                cols = slice((2 * j + mode) * size, (2 * j + mode + 1) * size)
                for part in range(2):
                    psis[j, part, mode, own, :] = psi[part]
                    high, low = split(psi[part])
                    in_high[pl.ds(part * size + first, ROWS), cols] = high
                    in_low[pl.ds(part * size + first, ROWS), cols] = low
        mean = jnp.sum(jnp.sum(norm, axis=0, keepdims=True), axis=1, keepdims=True) / (size * size)
        scales[j] = jnp.broadcast_to(1.0 / (mean + EPSILON), (8, size))

    wide = many * 2 * size
    yield

    def left(high, low, x_high, x_low):
        table = jnp.concatenate([high, high, low], axis=1)
        h = x_high[:, :wide]
        return jnp.dot(table, jnp.concatenate([h, x_low[:, :wide], h], axis=0), preferred_element_type=jnp.float32)

    def right(high, low, x_high, x_low):
        table = jnp.concatenate([high, high, low], axis=0)
        h = x_high[:wide, :]
        return jnp.dot(jnp.concatenate([h, x_low[:wide, :], h], axis=1), table, preferred_element_type=jnp.float32)

    half = left(minus_high, minus_low, in_high, in_low)
    yield
    for j in range(many):
        for mode in range(2):
            k = (2 * j + mode) * size
            for part in range(2):
                for first in range(0, size, ROWS):
                    value = half[part * size + first : part * size + first + ROWS, k : k + size]
                    high, low = split(value)
                    where = (pl.ds(k + first, ROWS), slice(part * size, (part + 1) * size))
                    row_high[where] = high
                    row_low[where] = low
    yield
    spectrum = right(plus_high, plus_low, row_high, row_low)
    yield
    for j, slot in enumerate(slots):
        for first in range(0, size, ROWS):
            values = {}
            for mode in range(2):
                k = (2 * j + mode) * size + first
                for part in range(2):
                    values[mode, part] = spectrum[k : k + ROWS, part * size : (part + 1) * size]
            total = sum(value**2 for value in values.values())
            factor = amp_ref[slot, pl.ds(first, ROWS), :] * lax.rsqrt(jnp.maximum(total, 1.0))
            for (mode, part), value in values.items():
                high, low = split(value * factor)
                where = (pl.ds((2 * j + mode) * size + first, ROWS), slice(part * size, (part + 1) * size))
                spec_high[where] = high
                spec_low[where] = low
    yield
    half = right(minus_high, minus_low, spec_high, spec_low)
    yield
    for j in range(many):
        for mode in range(2):
            k = (2 * j + mode) * size
            for part in range(2):
                for first in range(0, size, ROWS):
                    value = half[k + first : k + first + ROWS, part * size : (part + 1) * size]
                    high, low = split(value)
                    where = (pl.ds(part * size + first, ROWS), slice(k, k + size))
                    back_high[where] = high
                    back_low[where] = low
    yield
    revised = left(plus_high, plus_low, back_high, back_low)
    yield
    for first in range(0, size, ROWS):
        own = pl.ds(first, ROWS)
        gradient = {}
        for j, (row, tile, shift) in enumerate(places):
            scale = jnp.concatenate([scales[j]] * (ROWS // 8), axis=0)
            window = [windows[j, part, own, :] for part in range(2)]
            scaled = [value * scale for value in window]
            numer_real = numer_imag = 0.0
            for mode in range(2):
                k = (2 * j + mode) * size
                real = revised[first : first + ROWS, k : k + size] - psis[j, 0, mode, own, :]
                imag = revised[size + first : size + first + ROWS, k : k + size] - psis[j, 1, mode, own, :]
                p_real, p_imag = probe_ref[0, mode, own, :], probe_ref[1, mode, own, :]
                numer_real += p_real * real + p_imag * imag
                numer_imag += p_real * imag - p_imag * real
                gradient[0, mode] = gradient.get((0, mode), 0.0) + (scaled[0] * real + scaled[1] * imag)
                gradient[1, mode] = gradient.get((1, mode), 0.0) + (scaled[0] * imag - scaled[1] * real)
            add_rolled(sums_ref, 0, row + first, tile, shift, lane, numer_real)
            add_rolled(sums_ref, 1, row + first, tile, shift, lane, numer_imag)
        for (part, mode), value in gradient.items():
            gradient_ref[part, mode, own, :] += value


def handle(slots, margin, base, offset_ref, amp, probe, table, source, sums, gradient, work):
    chains = []
    at = 0
    for number, length in enumerate(split_of(len(slots))):
        mine = [ref.at[number] for ref in work]
        chains.append(stages(slots[at : at + length], margin, base, offset_ref, amp, probe, table, source, sums, gradient, mine))
        at += length
    live = list(enumerate(chains))
    step = 0
    while live:
        for item in list(live):
            if step >= item[0] * SKEW:
                try:
                    next(item[1])
                except StopIteration:
                    live.remove(item)
        step += 1


def weight_kernel(margin, count_ref, offset_ref, probe_ref, weight_ref, power_ref):
    size = probe_ref.shape[-1]
    weight_ref[...] = jnp.zeros_like(weight_ref)
    power_ref[...] = jnp.sum(probe_ref[...] ** 2, axis=(0, 1))
    lane = lax.broadcasted_iota(jnp.int32, (ROWS, size), 1)

    def visit(slot, carry):
        row, tile, shift = corner(offset_ref, slot, margin, 0, size)
        for first in range(0, size, ROWS):
            add_rolled(weight_ref, 0, row + first, tile, shift, lane, power_ref[pl.ds(first, ROWS), :])
        return carry

    lax.fori_loop(0, count_ref[0, 0], visit, 0)


def run_slots(margin, side, count_ref, offset_ref, chosen, *rest):
    size = 2 * margin

    def look(slot, found):
        left = offset_ref[slot, 1] + margin < size
        chosen[found] = slot
        return found + jnp.where(left, 1 - side, side)

    found = lax.fori_loop(0, count_ref[0, 0], look, 0)

    def group(i, carry):
        handle([chosen[PER * i + k] for k in range(PER)], margin, side, offset_ref, *rest)
        return carry

    lax.fori_loop(0, found // PER, group, 0)
    for left_over in range(1, PER):

        @pl.when(lax.rem(found, PER) == left_over)
        def _():
            first = found - left_over
            handle([chosen[first + k] for k in range(left_over)], margin, side, offset_ref, *rest)


def lanes_of(shape):
    return lax.broadcasted_iota(jnp.int32, shape, len(shape) - 1)


def turned(value, margin):
    return pltpu.roll(value, margin, 1)


def joined(low, high, margin):
    return jnp.where(lanes_of(low.shape) < margin, turned(low, margin), turned(high, margin))


def packed_low(real, imag, margin):
    return jnp.where(lanes_of(real.shape) < margin, real, turned(imag, margin))


def packed_high(real, imag, margin):
    return jnp.where(lanes_of(real.shape) < margin, turned(real, margin), imag)


def chosen_by(flag, first, second):
    return jnp.where(jnp.full(first.shape, flag, jnp.int32) == 1, first, second)


def extend_kernel(margin, flag_ref, object_ref, a_ref, b_ref, ext_ref, high_ref, low_ref):
    odd = lax.rem(flag_ref[0], 2)
    rows, cols = object_ref.shape[1:]
    size = 2 * margin
    blocks = cols // size
    segments = [(0, margin), (margin, rows), (margin + rows, margin)]
    for number, (first, length) in enumerate(segments):
        where = pl.ds(first, length)
        values = {}
        for part in range(2):
            for block in range(blocks):
                lanes = slice(block * size, (block + 1) * size)
                if number == 0:
                    value = chosen_by(odd, a_ref[part, :, lanes], b_ref[part, :, lanes])
                elif number == 1:
                    value = object_ref[part, :, lanes]
                else:
                    value = chosen_by(odd, b_ref[part, :, lanes], a_ref[part, :, lanes])
                values[part, block] = value
            zero = jnp.zeros((length, size), jnp.float32)
            for tile in range(blocks + 1):
                low = values.get((part, tile - 1), zero)
                high = values.get((part, tile), zero)
                ext_ref[tile, part, where, :] = joined(low, high, margin)
        high_ref[where, :] = packed_high(values[0, blocks - 1], values[1, blocks - 1], margin)
        low_ref[where, :] = packed_low(values[0, 0], values[1, 0], margin)


def first_left_kernel(margin, count, offset, amp, probe, table, ext, halo, weight, message, middle, gradient, ext_left, *work):
    source, sums, chosen, *work = work
    gradient[...] = jnp.zeros_like(gradient)
    sums[...] = jnp.zeros_like(sums)
    edge = halo[...]
    for part, value in enumerate((edge, turned(edge, margin))):
        ext_left[part] = jnp.where(lanes_of(edge.shape) < margin, value, ext[0, part])
        source[0, part] = ext_left[part]
        source[1, part] = ext[1, part]
    run_slots(margin, 0, count, offset, chosen, amp, probe, table, source, sums, gradient, work)
    message[0:2] = sums[0]
    message[2] = weight[0, 0]
    middle[...] = sums[1]


def first_right_kernel(margin, count, offset, amp, probe, table, ext, halo, gradient_in, sums, gradient, ext_right, *work):
    source, chosen, *work = work
    tiles = ext.shape[0]
    gradient[...] = gradient_in[...]
    sums[...] = jnp.zeros_like(sums)
    edge = halo[...]
    for part, value in enumerate((turned(edge, margin), edge)):
        ext_right[part] = jnp.where(lanes_of(edge.shape) < margin, ext[tiles - 1, part], value)
        for tile in range(1, tiles - 1):
            source[tile - 1, part] = ext[tile, part]
        source[tiles - 2, part] = ext_right[part]
    run_slots(margin, 1, count, offset, chosen, amp, probe, table, source, sums, gradient, work)


def gather_kernel(margin, flag_ref, sums, middle, message, weight, received, total, a_ref, b_ref):
    size = 2 * margin
    tiles = total.shape[0]
    rows = total.shape[2]
    total[0] = message[...]
    for tile in range(1, tiles):
        for channel in range(3):
            value = sums[tile - 1, channel] if channel < 2 else weight[tile, 0]
            if tile == 1 and channel < 2:
                value += middle[channel]
            if tile == tiles - 1:
                value += received[channel]
            total[tile, channel] = value
    odd = lax.rem(flag_ref[0], 2)
    down = pl.multiple_of((1 - odd) * (rows - size), 8)
    up = pl.multiple_of(odd * (rows - size), 8)
    for tile in range(tiles):
        for channel in range(3):
            a_ref[tile, channel] = total[tile, channel, pl.ds(down, size), :]
            b_ref[tile, channel] = total[tile, channel, pl.ds(up, size), :]


def update_kernel(margin, flag_ref, probe, total, a_ref, b_ref, ext, ext_left, ext_right, ext_next, last, inverse):
    size = 2 * margin
    tiles, _, rows, _ = total.shape
    row_index, col_index, row_count, col_count = (flag_ref[i] for i in range(4))
    odd = lax.rem(row_index, 2)
    power = jnp.sum(probe[...] ** 2, axis=(0, 1))
    largest = jnp.max(jnp.max(power, axis=0, keepdims=True), axis=1, keepdims=True)
    regular = 0.1 * largest + EPSILON
    inner_rows, inner_cols = rows - size, (tiles - 1) * size
    for first, length in ((0, size), (size, rows - 2 * size), (rows - size, size)):
        where = pl.ds(first, length)
        row = lax.broadcasted_iota(jnp.int32, (length, size), 0) + (first - margin) + row_index * inner_rows
        for tile in range(tiles):
            col = lanes_of((length, size)) + (tile * size - margin) + col_index * inner_cols
            inside = (row >= 0) & (row < row_count * inner_rows) & (col >= 0) & (col < col_count * inner_cols)
            values = [total[tile, channel, where, :] for channel in range(3)]
            for channel in range(3):
                if first == 0:
                    values[channel] += chosen_by(odd, a_ref[tile, channel], b_ref[tile, channel])
                elif first == rows - size:
                    values[channel] += chosen_by(odd, b_ref[tile, channel], a_ref[tile, channel])
            over = 1.0 / (values[2] + regular)
            inverse[tile, where, :] = over
            for part in range(2):
                if tile == 0:
                    before = ext_left[part, where, :]
                elif tile == tiles - 1:
                    before = ext_right[part, where, :]
                else:
                    before = ext[tile, part, where, :]
                after = jnp.where(inside, before + values[part] * over, 0.0)
                ext_next[tile, part, where, :] = after
                if tile == tiles - 1:
                    last[part, where, :] = after


def second_right_kernel(margin, count, offset, amp, probe, table, ext, gradient_in, inverse, sums, gradient, message, *work):
    source, chosen, *work = work
    tiles = ext.shape[0]
    gradient[...] = gradient_in[...]
    sums[...] = jnp.zeros_like(sums)
    source[...] = ext[1:]
    run_slots(margin, 1, count, offset, chosen, amp, probe, table, source, sums, gradient, work)
    message[0] = packed_high(sums[tiles - 2, 0], sums[tiles - 2, 1], margin)
    message[1] = inverse[tiles - 1]


def second_left_kernel(
    margin, count, offset, amp, probe, table, flag_ref, ext, received, gradient_in, sums, message, kept, sent, first, *work
):
    source, gradient, chosen, *work = work
    gradient[...] = gradient_in[...]
    sums[...] = jnp.zeros_like(sums)
    inward = jnp.minimum(flag_ref[1], 1)
    for part in range(2):
        first[part] = chosen_by(inward, received[part], ext[0, part])
        source[0, part] = first[part]
        source[1, part] = ext[1, part]
    run_slots(margin, 0, count, offset, chosen, amp, probe, table, source, sums, gradient, work)
    message[...] = packed_low(sums[0, 0], sums[0, 1], margin)
    odd = lax.rem(flag_ref[0], 2)
    kept[...] = gradient[odd]
    sent[...] = gradient[1 - odd]


def collect_kernel(margin, flag_ref, left, right, from_left, from_right, ext, first, inverse, inner, a_ref, b_ref, base, inv):
    size = 2 * margin
    tiles = ext.shape[0]
    rows = ext.shape[2]
    tall = rows - size
    inward = jnp.minimum(flag_ref[1], 1)
    for part in range(2):
        for block in range(tiles - 1):
            lanes = slice(block * size, (block + 1) * size)

            def tile_sum(tile):
                if tile == 0:
                    return left[0, part]
                return left[1, part] + right[0, part] if tile == 1 else right[tile - 1, part]

            value = joined(tile_sum(block), tile_sum(block + 1), margin)
            lane = lanes_of(value.shape)
            if block == 0:
                edge = from_left[0] if part == 0 else turned(from_left[0], margin)
                value += jnp.where(lane < margin, edge, 0.0)
            if block == tiles - 2:
                edge = turned(from_right[...], margin) if part == 0 else from_right[...]
                value += jnp.where(lane < margin, 0.0, edge)
            inner[part, :, lanes] = value
            own = pl.ds(margin, tall)
            low = first[part, own, :] if block == 0 else ext[block, part, own, :]
            base[part, :, lanes] = joined(low, ext[block + 1, part, own, :], margin)
            if part == 0:
                low = inverse[block, own, :]
                if block == 0:
                    low = chosen_by(inward, from_left[1, own, :], low)
                inv[:, lanes] = joined(low, inverse[block + 1, own, :], margin)
    odd = lax.rem(flag_ref[0], 2)
    down = pl.multiple_of((1 - odd) * (rows - margin), 8)
    up = pl.multiple_of(odd * (rows - margin), 8)
    for part in range(2):
        a_ref[part] = inner[part, pl.ds(down, margin), :]
        b_ref[part] = inner[part, pl.ds(up, margin), :]


def finish_kernel(margin, flag_ref, inner, a_ref, b_ref, base, inv, out):
    odd = lax.rem(flag_ref[0], 2)
    rows = base.shape[1]
    for part in range(2):
        for first, length in ((0, margin), (margin, rows - 2 * margin), (rows - margin, margin)):
            value = inner[part, pl.ds(margin + first, length), :]
            if first == 0:
                value += chosen_by(odd, a_ref[part], b_ref[part])
            elif first == rows - margin:
                value += chosen_by(odd, b_ref[part], a_ref[part])
            where = pl.ds(first, length)
            out[part, where, :] = base[part, where, :] + value * inv[where, :]


def call(kernel, shapes, arguments, scalars, scratch=(), flops=10**7):
    def space(is_scalar):
        return pl.BlockSpec(memory_space=pltpu.SMEM if is_scalar else pltpu.VMEM)

    return pl.pallas_call(
        kernel,
        out_shape=[jax.ShapeDtypeStruct(shape, jnp.float32) for shape in shapes],
        in_specs=[space(i in scalars) for i in range(len(arguments))],
        out_specs=[space(False)] * len(shapes),
        scratch_shapes=list(scratch),
        compiler_params=pltpu.CompilerParams(vmem_limit_bytes=VMEM_BYTES),
        cost_estimate=pl.CostEstimate(flops=flops, bytes_accessed=10**6, transcendentals=0),
    )(*arguments)


def work_scratch(size):
    bf16 = jnp.bfloat16
    n = max(split_of(PER))
    c = len(split_of(PER))
    tall = pltpu.VMEM((c, n * 2 * size, 2 * size), bf16)
    wide = pltpu.VMEM((c, 2 * size, n * 2 * size), bf16)
    return [
        pltpu.VMEM((c, n, 2, size, size), jnp.float32),
        pltpu.VMEM((c, n, 2, 2, size, size), jnp.float32),
        wide, wide, tall, tall, tall, tall, wide, wide,
        pltpu.VMEM((c, n, 8, size), jnp.float32),
    ]


def shifted(value, axis, steps):
    count = lax.axis_size(axis)
    initial, last = max(0, -steps), min(count, count - steps)
    return lax.ppermute(value, axis, [(source, source + steps) for source in range(initial, last)])


def swapped(value, axis, first):
    pairs = []
    for i in range(first, lax.axis_size(axis) - 1, 2):
        pairs += [(i, i + 1), (i + 1, i)]
    return lax.ppermute(value, axis, pairs)


def all_sum(total):
    cols = lax.axis_size("col")
    count = lax.axis_size("row") * cols
    masks = []
    distance = 2
    while distance < lax.axis_size("row"):
        masks.append(distance * cols)
        distance *= 2
    distance = 1
    while distance < cols:
        masks.append(distance)
        distance *= 2

    def partner(mask):
        return lax.ppermute(total, ("row", "col"), [(i, i ^ mask) for i in range(count)])

    while masks:
        near, *masks = masks
        if masks:
            far, *masks = masks
            one, two, three = partner(near), partner(far), partner(near ^ far)
            total = (total + one) + (two + three)
        else:
            total = total + partner(near)
    return total


def local(object_field, probe, amplitudes, offsets, counts):
    size = probe.shape[2]
    margin = size // 2
    slot_total = amplitudes.shape[2]
    amplitudes, offsets = amplitudes[0, 0], offsets[0, 0]
    table = tables(size)
    tile_rows, tile_cols = object_field.shape[1:]
    rows = tile_rows + size
    tiles = tile_cols // size + 1
    row_index, col_index = lax.axis_index("row"), lax.axis_index("col")
    flags = jnp.stack([row_index, col_index, lax.axis_size("row"), lax.axis_size("col")]).astype(jnp.int32)
    odd = row_index % 2 == 1

    upper, lower = object_field[:, :margin], object_field[:, -margin:]
    a_in = swapped(jnp.where(odd, upper, lower), "row", 0)
    b_in = swapped(jnp.where(odd, lower, upper), "row", 1)

    weight, _ = call(
        functools.partial(weight_kernel, margin),
        [(tiles, 1, rows, size), (size, size)],
        [counts, offsets, probe],
        (0, 1),
    )
    ext, high, low = call(
        functools.partial(extend_kernel, margin),
        [(tiles, 2, rows, size), (rows, size), (rows, size)],
        [flags, object_field, a_in, b_in],
        (0,),
    )
    left_halo = shifted(high, "col", 1)
    right_halo = shifted(low, "col", -1)

    common = [counts, offsets, amplitudes, probe, table]
    list_scratch = pltpu.SMEM((slot_total + 1,), jnp.int32)
    work = work_scratch(size)
    two_tiles = pltpu.VMEM((2, 2, rows, size), jnp.float32)
    right_tiles = pltpu.VMEM((tiles - 1, 2, rows, size), jnp.float32)
    column = (2, rows, size)
    heavy = 4 * 10**10

    message, middle, gradient, ext_left = call(
        functools.partial(first_left_kernel, margin),
        [(3, rows, size), column, probe.shape, column],
        common + [ext, left_halo, weight],
        (0, 1),
        [two_tiles, two_tiles, list_scratch] + work,
        heavy,
    )
    from_right = shifted(message, "col", -1)
    sums, gradient, ext_right = call(
        functools.partial(first_right_kernel, margin),
        [(tiles - 1,) + column, probe.shape, column],
        common + [ext, right_halo, gradient],
        (0, 1),
        [right_tiles, list_scratch] + work,
        heavy,
    )
    total, a_out, b_out = call(
        functools.partial(gather_kernel, margin),
        [(tiles, 3, rows, size), (tiles, 3, size, size), (tiles, 3, size, size)],
        [flags, sums, middle, message, weight, from_right],
        (0,),
    )
    a_in = swapped(a_out, "row", 0)
    b_in = swapped(b_out, "row", 1)
    ext, last, inverse = call(
        functools.partial(update_kernel, margin),
        [(tiles,) + column, column, (tiles, rows, size)],
        [flags, probe, total, a_in, b_in, ext, ext_left, ext_right],
        (0,),
    )
    from_left = shifted(last, "col", 1)
    right, gradient, message = call(
        functools.partial(second_right_kernel, margin),
        [(tiles - 1,) + column, probe.shape, column],
        common + [ext, gradient, inverse],
        (0, 1),
        [right_tiles, list_scratch] + work,
        heavy,
    )
    edge_left = shifted(message, "col", 1)
    left, message, kept, sent, first = call(
        functools.partial(second_left_kernel, margin),
        [(2,) + column, (rows, size), probe.shape[1:], probe.shape[1:], column],
        common + [flags, ext, from_left, gradient],
        (0, 1, 5),
        [two_tiles, pltpu.VMEM(probe.shape, jnp.float32), list_scratch] + work,
        heavy,
    )
    edge_right = shifted(message, "col", -1)
    share = all_sum(kept + swapped(sent, "row", 0))

    wide = (2, rows, tile_cols)
    inner, a_out, b_out, base, inv = call(
        functools.partial(collect_kernel, margin),
        [wide, (2, margin, tile_cols), (2, margin, tile_cols), object_field.shape, object_field.shape[1:]],
        [flags, left, right, edge_left, edge_right, ext, first, inverse],
        (0,),
    )
    a_in = swapped(a_out, "row", 0)
    b_in = swapped(b_out, "row", 1)
    (object_next,) = call(
        functools.partial(finish_kernel, margin),
        [object_field.shape],
        [flags, inner, a_in, b_in, base, inv],
        (0,),
    )

    divisor = float(lax.axis_size("row") * lax.axis_size("col") * slot_total)
    share = jnp.where(odd, probe[1], probe[0]) + share / divisor
    other = swapped(share, "row", 0)
    probe_next = jnp.where(odd, jnp.stack([other, share]), jnp.stack([share, other]))
    return object_next, probe_next


def solution(mesh):
    in_specs = (
        P(None, "row", "col"),
        P(),
        P("row", "col", None, None, None),
        P("row", "col", None, None),
        P("row", "col"),
    )
    out_specs = (P(None, "row", "col"), P())
    return jax.shard_map(local, mesh=mesh, in_specs=in_specs, out_specs=out_specs, check_vma=False)
```
